128 devices in a mesh: replica: 32 (over y, z, x_hi), tensor: 4 (over x_lo, core).
Axes of the slice: x: 4 (x_hi: 2, x_lo: 2; x = x_hi * 2 + x_lo), y: 4, z: 4, core: 2. Of those that a mesh axis runs over, the one named last changes fastest.
Arguments:
- gate_pre: bfloat16 [32, 512, 7168], P('replica', None, 'tensor'), may hold values from -6 to 6
- up_pre: bfloat16 [32, 512, 7168], P('replica', None, 'tensor'), may hold values from -6 to 6
- down_weight: bfloat16 [32, 7168, 2560], P('replica', 'tensor'), may hold values from -6 to 6
- cotangent: bfloat16 [32, 512, 2560], P('replica', 'tensor'), may hold values from -6 to 6
- peer_exp: int32 [1], replicated, may hold values from 0 to 4
Outputs:
- layer_out: bfloat16 [32, 512, 2560], P('replica', 'tensor')
- grad_gate: bfloat16 [32, 512, 7168], P('replica', None, 'tensor')
- grad_up: bfloat16 [32, 512, 7168], P('replica', None, 'tensor')
- mixed_weight: bfloat16 [32, 7168, 2560], P('replica', 'tensor')
The draws below stay inside these ranges and needn't reach their ends.
Inputs may be any that keep to these rules, and one draw needn't show every extreme that they name: `peer_exp`: one value for all replicas.
All inputs are finite; a program needn't handle non-finite values.
Results may differ from the reference program's by a relative error of at most 0.0052.
Values may be sent and summed in bfloat16 or wider, within the bound.
No kernel may reach another device: no remote copies, remote signals or barrier semaphores. Data moves between devices by JAX's collectives and lax.ppermute only.
A program may use at most 128 MiB of HBM per device.

```python
import jax
import jax.numpy as jnp
from jax import lax

D = 2560
FF = 7168
TOK = 512
REPLICAS = 32


def block_levels(key, extent, shards, least, high):
    gain = 1.0
    for axis_at, blocks in shards:
        heights = jax.random.uniform(jax.random.fold_in(jax.random.fold_in(key, 6), axis_at), (blocks,), jnp.float32, least / len(shards), high / len(shards))
        gain = gain * jnp.repeat(jnp.exp(heights), extent[axis_at] // blocks).reshape((-1,) + (1,) * (len(extent) - 1 - axis_at))
    return gain


def noise(rng, dims, deviation, reach, shards=(), held_as=jnp.bfloat16):
    gain = block_levels(rng, dims, shards, -0.22, 0.18) if shards else 1.0
    array = jax.random.normal(rng, dims, jnp.float32) * deviation * gain
    return jnp.minimum(jnp.maximum(array, -reach), reach).astype(held_as)


def setup_inputs(seed: int = 0) -> dict:
    keys = jax.random.split(jax.random.key(seed), 6)
    gate_pre = noise(keys[0], (REPLICAS, TOK, FF), 1.0, 6.0, ((0, 32), (2, 4)))
    up_pre = noise(keys[1], (REPLICAS, TOK, FF), 1.0, 6.0, ((0, 32), (2, 4)))
    down_weight = noise(keys[2], (REPLICAS, FF, D), 1.0, 6.0, ((0, 32), (1, 4)))
    cotangent = noise(keys[3], (REPLICAS, TOK, D), 1.0, 6.0, ((0, 32), (1, 4)))
    peer_exp = jax.random.randint(keys[4], (1,), 0, 5).astype(jnp.int32)
    return {"gate_pre": gate_pre, "up_pre": up_pre, "down_weight": down_weight, "cotangent": cotangent, "peer_exp": peer_exp}


def one_replica(items):
    gate_pre, up_pre, weight, cot = items
    scale = 1.0 / jnp.sqrt(jnp.float32(weight.shape[0]))
    gate = gate_pre.astype(jnp.float32)
    upv = up_pre.astype(jnp.float32)
    sig = jax.nn.sigmoid(gate)
    act = gate * sig
    hidden = (act * upv).astype(jnp.bfloat16)
    layer_out = (jnp.dot(hidden, weight, preferred_element_type=jnp.float32) * scale).astype(jnp.bfloat16)
    grad_hidden = jnp.dot(cot, weight.T, preferred_element_type=jnp.float32) * scale
    grad_gate = (grad_hidden * upv * sig * (1.0 + gate * (1.0 - sig))).astype(jnp.bfloat16)
    grad_up = (grad_hidden * act).astype(jnp.bfloat16)
    weight_grad = jnp.dot(hidden.T, cot, preferred_element_type=jnp.float32) * scale
    updated = (weight.astype(jnp.float32) - 2.0 * weight_grad).astype(jnp.bfloat16)
    return (layer_out, grad_gate, grad_up, updated)

def reference(gate_pre, up_pre, down_weight, cotangent, peer_exp):
    layer_out, grad_gate, grad_up, updated = lax.map(one_replica, (gate_pre, up_pre, down_weight, cotangent))
    distance = jnp.left_shift(jnp.int32(1), peer_exp[0].astype(jnp.int32)) % updated.shape[0]
    peer = jnp.roll(updated, distance, axis=0)
    mixed_weight = ((updated.astype(jnp.float32) + peer.astype(jnp.float32)) * 0.5).astype(jnp.bfloat16)
    return (layer_out, grad_gate, grad_up, mixed_weight)
```

```python
import functools

import jax
import jax.numpy as jnp
import numpy as np
from jax import lax
from jax.experimental import pallas as pl
from jax.experimental.pallas import tpu as pltpu
from jax.sharding import PartitionSpec as P

learning_rate = 2.0
both = ("replica", "tensor")
vmem = 56 * 2**20
head = 768
head_cuts = (256, 256, 256)
even_cuts = (768, 512, 512)
odd_cuts = (384, 384, 512, 512)
cost_cut = 100
grads_wide = 256
params = pltpu.CompilerParams(vmem_limit_bytes=vmem)


def place(x, y, z, core):
    replica = (y % 4) * 8 + (z % 4) * 2 + (x % 4) // 2
    return replica * 4 + (x % 2) * 2 + core


def chips():
    return [(x, y, z, core) for x in range(4) for y in range(4) for z in range(4) for core in range(2)]


def direct_pairs(power):
    distance = 2**power
    return [
        (r * 4 + t, ((r + distance) % 32) * 4 + t) for r in range(32) for t in range(4)
    ]


def backward_hops(power):
    if power == 3:
        step = [(place(x, y, z, c), place(x, y - 1, z, c)) for x, y, z, c in chips()]
        return [step, step, step]
    step = [(place(x, y, z, c), place(x, y, z - 1, c)) for x, y, z, c in chips()]
    last = [
        (place(x, y, z, c), place(x, y + (1 if z == 1 else 0), z - 1, c))
        for x, y, z, c in chips()
    ]
    return [step, step, last]


def swapped(value, mask):
    return lax.ppermute(value, "tensor", [(t, t ^ mask) for t in range(4)])


def estimate(flops, read):
    return pl.CostEstimate(flops=flops // cost_cut, bytes_accessed=read // cost_cut, transcendentals=0)


def in_rows(count, step, body):
    def one(i, carry):
        body(pl.ds(pl.multiple_of(i * step, step), step))
        return carry

    lax.fori_loop(0, count // step, one, 0)


def hidden_kernel(gate_ref, up_ref, hidden_ref):
    def body(rows):
        gate = gate_ref[rows, :].astype(jnp.float32)
        up = up_ref[rows, :].astype(jnp.float32)
        hidden_ref[rows, :] = (gate * jax.nn.sigmoid(gate) * up).astype(jnp.bfloat16)

    in_rows(gate_ref.shape[0], 64, body)


def make_hidden(gate, up):
    tokens, units = gate.shape
    block = pl.BlockSpec((tokens, units // 2), lambda i: (0, i))
    return pl.pallas_call(
        hidden_kernel,
        grid=(2,),
        in_specs=[block, block],
        out_specs=block,
        out_shape=jax.ShapeDtypeStruct((tokens, units), jnp.bfloat16),
        compiler_params=params,
        cost_estimate=estimate(tokens * units * 10, tokens * units * 6),
    )(gate, up)


def put_tokens(at_ref, part_refs, whole_ref, lo):
    size, wide = part_refs[0].shape
    for mask, part in enumerate(part_refs):
        row = pl.multiple_of((at_ref[0] ^ mask) * size, size)
        whole_ref[pl.ds(row, size), lo : lo + wide] = part[...]


def updated_kernel(factor, first, cuts, at_ref, own, core, chip, far, hidden_ref, weight_ref, *refs):
    out_refs, cot_ref = refs[:-1], refs[-1]

    @pl.when(pl.program_id(0) == 0)
    def _():
        put_tokens(at_ref, (own, core, chip, far), cot_ref, 0)

    at = 0
    for out_ref, width in zip(out_refs, cuts):
        total = lax.dot_general(
            hidden_ref[...],
            cot_ref[:, at : at + width],
            (((0,), (0,)), ((), ())),
            preferred_element_type=jnp.float32,
        )
        old = weight_ref[:, first + at : first + at + width].astype(jnp.float32)
        out_ref[...] = (old - factor * total).astype(jnp.bfloat16)
        at += width


def make_updated(at, parts, hidden, weight, factor, first, cuts):
    tokens, units = hidden.shape
    rows = units // 2 if first == 0 else 256
    wide = sum(cuts)
    columns = wide if first == 0 else weight.shape[1]
    part = pl.BlockSpec(parts[0].shape, lambda i, at: (0, 0))
    return pl.pallas_call(
        functools.partial(updated_kernel, factor, first, cuts),
        grid_spec=pltpu.PrefetchScalarGridSpec(
            num_scalar_prefetch=1,
            grid=(units // rows,),
            in_specs=[part] * 4
            + [
                pl.BlockSpec((tokens, rows), lambda i, at: (0, i)),
                pl.BlockSpec((rows, columns), lambda i, at: (i, 0)),
            ],
            out_specs=[pl.BlockSpec((rows, width), lambda i, at: (i, 0)) for width in cuts],
            scratch_shapes=[pltpu.VMEM((tokens, wide), jnp.bfloat16)],
        ),
        out_shape=[jax.ShapeDtypeStruct((units, width), jnp.bfloat16) for width in cuts],
        compiler_params=params,
        cost_estimate=estimate(2 * units * tokens * wide, units * (columns + wide) * 2),
    )(at, *parts, hidden, weight)


def terms_kernel(scale, at_ref, hidden_ref, weight_ref, keep_ref, send_ref, total_ref):
    def body(rows):
        total_ref[rows, :] = scale * jnp.dot(
            hidden_ref[rows, :], weight_ref[...], preferred_element_type=jnp.float32
        )

    in_rows(total_ref.shape[0], 256, body)
    size = keep_ref.shape[1]
    for chip in range(2):
        for out_ref, mask in ((keep_ref, 2 * chip), (send_ref, 2 * chip + 1)):
            row = pl.multiple_of((at_ref[0] ^ mask) * size, size)
            out_ref[chip] = total_ref[pl.ds(row, size), :]


def make_terms(at, hidden, weight, scale):
    tokens, units = hidden.shape
    features = weight.shape[1]
    size = tokens // 4
    block = pl.BlockSpec((2, size, 512), lambda i, at: (0, 0, i))
    shape = jax.ShapeDtypeStruct((2, size, features), jnp.float32)
    return pl.pallas_call(
        functools.partial(terms_kernel, scale),
        grid_spec=pltpu.PrefetchScalarGridSpec(
            num_scalar_prefetch=1,
            grid=(features // 512,),
            in_specs=[
                pl.BlockSpec((tokens, units), lambda i, at: (0, 0)),
                pl.BlockSpec((units, 512), lambda i, at: (0, i)),
            ],
            out_specs=[block, block],
            scratch_shapes=[pltpu.VMEM((tokens, 512), jnp.float32)],
        ),
        out_shape=[shape, shape],
        compiler_params=params,
        cost_estimate=estimate(2 * units * tokens * features, units * features * 2 + tokens * features * 4),
    )(at, hidden, weight)


def chip_sum_kernel(keep_ref, sibling_ref, out_ref):
    def body(rows):
        out_ref[rows, :] = (keep_ref[0, rows, :] + sibling_ref[0, rows, :]).astype(out_ref.dtype)

    in_rows(out_ref.shape[0], 16, body)


def chip_sum(keep, sibling, kind):
    _, size, features = keep.shape
    block = pl.BlockSpec((1, size, features), lambda i: (1, 0, 0))
    return pl.pallas_call(
        chip_sum_kernel,
        grid=(1,),
        in_specs=[block, block],
        out_specs=pl.BlockSpec((size, features), lambda i: (0, 0)),
        out_shape=jax.ShapeDtypeStruct((size, features), kind),
        compiler_params=params,
        cost_estimate=estimate(size * features, size * features * 12),
    )(keep, sibling)


def last_sum_kernel(keep_ref, sibling_ref, other_ref, out_ref):
    def body(rows):
        total = keep_ref[0, rows, :] + sibling_ref[0, rows, :]
        out_ref[rows, :] = (total + other_ref[rows, :].astype(jnp.float32)).astype(jnp.bfloat16)

    in_rows(out_ref.shape[0], 16, body)


def last_sum(keep, sibling, other):
    _, size, features = keep.shape
    block = pl.BlockSpec((1, size, features), lambda i: (0, 0, 0))
    flat = pl.BlockSpec((size, features), lambda i: (0, 0))
    return pl.pallas_call(
        last_sum_kernel,
        grid=(1,),
        in_specs=[block, block, flat],
        out_specs=flat,
        out_shape=jax.ShapeDtypeStruct((size, features), jnp.bfloat16),
        compiler_params=params,
        cost_estimate=estimate(2 * size * features, size * features * 14),
    )(keep, sibling, other)


def grads_kernel(scale, at_ref, *refs):
    head_refs, rest_refs = refs[:4], refs[4:8]
    weight_ref, gate_ref, up_ref, gate_out, up_out, cot_ref, total_ref = refs[8:]

    @pl.when(pl.program_id(0) == 0)
    def _():
        put_tokens(at_ref, head_refs, cot_ref, 0)
        put_tokens(at_ref, rest_refs, cot_ref, head)

    def product(rows):
        total_ref[rows, :] = scale * lax.dot_general(
            cot_ref[rows, :], weight_ref[...], (((1,), (1,)), ((), ())), preferred_element_type=jnp.float32
        )

    in_rows(total_ref.shape[0], 256, product)

    def body(rows):
        total = total_ref[rows, :]
        gate = gate_ref[rows, :].astype(jnp.float32)
        up = up_ref[rows, :].astype(jnp.float32)
        sig = jax.nn.sigmoid(gate)
        gate_out[rows, :] = (total * up * sig * (1.0 + gate * (1.0 - sig))).astype(jnp.bfloat16)
        up_out[rows, :] = (total * (gate * sig)).astype(jnp.bfloat16)

    in_rows(gate_ref.shape[0], 64, body)


def make_grads(at, head_parts, rest_parts, weight, gate, up, scale):
    tokens, units = gate.shape
    features = weight.shape[1]
    wide = grads_wide
    block = pl.BlockSpec((tokens, wide), lambda i, at: (0, i))
    shape = jax.ShapeDtypeStruct((tokens, units), jnp.bfloat16)
    parts = list(head_parts) + list(rest_parts)
    return pl.pallas_call(
        functools.partial(grads_kernel, scale),
        grid_spec=pltpu.PrefetchScalarGridSpec(
            num_scalar_prefetch=1,
            grid=(units // wide,),
            in_specs=[pl.BlockSpec(part.shape, lambda i, at: (0, 0)) for part in parts]
            + [pl.BlockSpec((wide, features), lambda i, at: (i, 0)), block, block],
            out_specs=[block, block],
            scratch_shapes=[
                pltpu.VMEM((tokens, features), jnp.bfloat16),
                pltpu.VMEM((tokens, wide), jnp.float32),
            ],
        ),
        out_shape=[shape, shape],
        compiler_params=params,
        cost_estimate=estimate(2 * units * tokens * features, units * features * 2 + tokens * units * 8),
    )(at, *parts, weight, gate, up)


def averaged_kernel(own_ref, peer_ref, *refs):
    out_ref = refs[-1]

    def body(rows):
        own = own_ref[rows, :].astype(jnp.float32)
        out_ref[rows, :] = ((own + peer_ref[rows, :].astype(jnp.float32)) * 0.5).astype(jnp.bfloat16)

    in_rows(out_ref.shape[0], 64, body)


def averaged(mixed, own, peer, at, features):
    units, width = own.shape
    assert at % width == 0
    block = pl.BlockSpec((units // 2, width), lambda i: (i, 0))
    place_at = at // width
    before = [] if mixed is None else [mixed]
    return pl.pallas_call(
        averaged_kernel,
        grid=(2,),
        in_specs=[block, block] + [pl.BlockSpec(memory_space=pl.ANY)] * len(before),
        out_specs=pl.BlockSpec((units // 2, width), lambda i: (i, place_at)),
        out_shape=jax.ShapeDtypeStruct((units, features), jnp.bfloat16),
        input_output_aliases={2: 0} if before else {},
        compiler_params=params,
        cost_estimate=estimate(units * width * 2, units * width * 6),
    )(own, peer, *before)


def step_with(power, scale, at, gate, up, weight, head_parts, rest_rows, rest_core, hidden, new_head):
    features = weight.shape[1]
    factor = learning_rate * scale
    odd = power in (1, 3)
    rest_cuts = odd_cuts if odd else even_cuts
    around, order = ((2, 3), (0, 1, 4, 2, 5, 3, 6)) if odd else ((), (0, 1, 3, 4, 5, 2))

    def hop(value, piece, count):
        if piece in around:
            return lax.ppermute(value, both, backward_hops(power)[count])
        return lax.ppermute(value, both, direct_pairs(power))

    hops = {piece: hop(new_head[piece], piece, 0) for piece in ((0, 1, 2) if odd else (0, 1))}

    chip = swapped(rest_rows, 2)
    keep, send = make_terms(at, hidden, weight, scale)
    hops[0], chip, keep, send = lax.optimization_barrier((hops[0], chip, keep, send))
    if odd:
        hops[2], chip = lax.optimization_barrier((hops[2], chip))
        hops[2] = hop(hops[2], 2, 1)
    rest_parts = (rest_rows, rest_core, chip, swapped(chip, 1))

    new_rest = list(make_updated(at, rest_parts, hidden, weight, factor, head, rest_cuts))
    if odd:
        hops[3] = hop(new_rest[0], 3, 0)
        hops[4] = hop(new_rest[1], 4, 0)
        hops[1], hops[2], new_rest[2], gate, send = lax.optimization_barrier(
            (hops[1], hops[2], new_rest[2], gate, send)
        )
        hops[2] = hop(hops[2], 2, 2)
        hops[5] = hop(new_rest[2], 5, 0)
        hops[3] = hop(hops[3], 3, 1)
        hops[4], new_rest[3] = lax.optimization_barrier((hops[4], new_rest[3]))
        hops[6] = hop(new_rest[3], 6, 0)
        hops[2], hops[3] = lax.optimization_barrier((hops[2], hops[3]))
        hops[3] = hop(hops[3], 3, 2)
    else:
        hops[3] = hop(new_rest[0], 3, 0)
        hops[1], new_rest[1], send = lax.optimization_barrier((hops[1], new_rest[1], send))
        hops[4] = hop(new_rest[1], 4, 0)
        hops[3], new_rest[2], gate = lax.optimization_barrier((hops[3], new_rest[2], gate))
        hops[5] = hop(new_rest[2], 5, 0)
        hops[2] = hop(new_head[2], 2, 0)
    sibling = swapped(send, 1)
    grad_gate, grad_up = make_grads(at, head_parts, rest_parts, weight, gate, up, scale)
    kind = jnp.bfloat16 if power == 0 else jnp.float32
    layer_out = last_sum(keep, sibling, swapped(chip_sum(keep, sibling, kind), 2))

    pieces = list(new_head) + list(new_rest)
    starts = []
    column = 0
    for width in head_cuts + rest_cuts:
        starts.append(column)
        column += width
    mixed = None
    for count, piece in enumerate(order):
        value = hops[piece]
        if count == 3:
            value, layer_out = lax.optimization_barrier((value, layer_out))
        mixed = averaged(mixed, pieces[piece], value, starts[piece], features)
    return layer_out, grad_gate, grad_up, mixed


def per_device(gate_pre, up_pre, down_weight, cotangent, peer_exp):
    gate, up, weight, cot_rows = gate_pre[0], up_pre[0], down_weight[0], cotangent[0]
    width_all = weight.shape[0] * lax.axis_size("tensor")
    scale = float(np.float32(1.0) / np.sqrt(np.float32(width_all)))
    at = lax.axis_index("tensor").astype(jnp.int32).reshape(1)

    rows = cot_rows[:, :head]
    rest_rows = cot_rows[:, head:]
    core = swapped(rows, 1)
    chip = swapped(rows, 2)
    hidden = make_hidden(gate, up)
    chip, hidden, rest_rows = lax.optimization_barrier((chip, hidden, rest_rows))
    head_parts = (rows, core, chip, swapped(chip, 1))
    rest_core = swapped(rest_rows, 1)
    new_head = make_updated(at, head_parts, hidden, weight, learning_rate * scale, 0, head_cuts)

    outs = lax.switch(
        jnp.clip(peer_exp[0], 0, 4),
        [functools.partial(step_with, power, scale) for power in range(5)],
        at,
        gate,
        up,
        weight,
        head_parts,
        rest_rows,
        rest_core,
        hidden,
        tuple(new_head),
    )
    return tuple(out[None] for out in outs)


def solution(mesh):
    return jax.shard_map(
        per_device,
        mesh=mesh,
        in_specs=(
            P("replica", None, "tensor"),
            P("replica", None, "tensor"),
            P("replica", "tensor", None),
            P("replica", "tensor", None),
            P(),
        ),
        out_specs=(
            P("replica", "tensor", None),
            P("replica", None, "tensor"),
            P("replica", None, "tensor"),
            P("replica", "tensor", None),
        ),
        check_vma=False,
    )
```

```python
import functools
import math

import jax
import jax.numpy as jnp
import numpy as np
from jax import lax
from jax.experimental import pallas as pl
from jax.experimental.pallas import tpu as pltpu
from jax.sharding import PartitionSpec as P

learning_rate = 2.0
both = ("replica", "tensor")
vmem = 56 * 2**20
head = 768
head_runs = ((0, 512), (512, 256), (0, 256), (256, 256))
even_cuts = (768, 512, 512)
odd_cuts = (384, 384, 1024)
cost_cut = 100
grads_wide = 256
params = pltpu.CompilerParams(vmem_limit_bytes=vmem)


def place(x, y, z, core):
    replica = (y % 4) * 8 + (z % 4) * 2 + (x % 4) // 2
    return replica * 4 + (x % 2) * 2 + core


def chips():
    return [(x, y, z, core) for x in range(4) for y in range(4) for z in range(4) for core in range(2)]


def direct_pairs(power):
    distance = 2**power
    return [
        (r * 4 + t, ((r + distance) % 32) * 4 + t) for r in range(32) for t in range(4)
    ]


def backward_hops(power):
    if power == 3:
        step = [(place(x, y, z, c), place(x, y - 1, z, c)) for x, y, z, c in chips()]
        return [step, step, step]
    step = [(place(x, y, z, c), place(x, y, z - 1, c)) for x, y, z, c in chips()]
    last = [
        (place(x, y, z, c), place(x, y + (1 if z == 1 else 0), z - 1, c))
        for x, y, z, c in chips()
    ]
    return [step, step, last]


def swapped(value, mask):
    return lax.ppermute(value, "tensor", [(t, t ^ mask) for t in range(4)])


def estimate(flops, read):
    return pl.CostEstimate(flops=flops // cost_cut, bytes_accessed=read // cost_cut, transcendentals=0)


def in_rows(count, step, body):
    def one(i, carry):
        body(pl.ds(pl.multiple_of(i * step, step), step))
        return carry

    lax.fori_loop(0, count // step, one, 0)


def hidden_kernel(gate_ref, up_ref, hidden_ref):
    def body(rows):
        gate = gate_ref[rows, :].astype(jnp.float32)
        up = up_ref[rows, :].astype(jnp.float32)
        hidden_ref[rows, :] = (gate * jax.nn.sigmoid(gate) * up).astype(jnp.bfloat16)

    in_rows(gate_ref.shape[0], 64, body)


def make_hidden(gate, up):
    tokens, units = gate.shape
    block = pl.BlockSpec((tokens, units // 2), lambda i: (0, i))
    return pl.pallas_call(
        hidden_kernel,
        grid=(2,),
        in_specs=[block, block],
        out_specs=block,
        out_shape=jax.ShapeDtypeStruct((tokens, units), jnp.bfloat16),
        compiler_params=params,
        cost_estimate=estimate(tokens * units * 10, tokens * units * 6),
    )(gate, up)


def put_tokens(at_ref, part_refs, whole_ref, lo):
    size, wide = part_refs[0].shape
    for mask, part in enumerate(part_refs):
        row = pl.multiple_of((at_ref[0] ^ mask) * size, size)
        whole_ref[pl.ds(row, size), lo : lo + wide] = part[...]


def updated_kernel(factor, first, runs, at_ref, own, core, chip, far, hidden_ref, weight_ref, *refs):
    out_refs, cot_ref = refs[:-1], refs[-1]

    @pl.when(pl.program_id(0) == 0)
    def _():
        put_tokens(at_ref, (own, core, chip, far), cot_ref, 0)

    made = []
    for out_ref, (at, width) in zip(out_refs, runs):
        inside = [(ref, at - lo) for ref, lo, size in made if lo <= at and at + width <= lo + size]
        made.append((out_ref, at, width))
        if inside:
            wider, skip = inside[0]
            out_ref[...] = wider[:, skip : skip + width]
            continue
        total = lax.dot_general(
            hidden_ref[...],
            cot_ref[:, at : at + width],
            (((0,), (0,)), ((), ())),
            preferred_element_type=jnp.float32,
        )
        old = weight_ref[:, first + at : first + at + width].astype(jnp.float32)
        out_ref[...] = (old - factor * total).astype(jnp.bfloat16)


def make_updated(at, parts, hidden, weight, factor, first, runs):
    tokens, units = hidden.shape
    rows = units // 2 if first == 0 else 256
    wide = parts[0].shape[1]
    cuts = [width for _, width in runs]
    columns = wide if first == 0 else weight.shape[1]
    part = pl.BlockSpec(parts[0].shape, lambda i, at: (0, 0))
    return pl.pallas_call(
        functools.partial(updated_kernel, factor, first, runs),
        grid_spec=pltpu.PrefetchScalarGridSpec(
            num_scalar_prefetch=1,
            grid=(units // rows,),
            in_specs=[part] * 4
            + [
                pl.BlockSpec((tokens, rows), lambda i, at: (0, i)),
                pl.BlockSpec((rows, columns), lambda i, at: (i, 0)),
            ],
            out_specs=[pl.BlockSpec((rows, width), lambda i, at: (i, 0)) for width in cuts],
            scratch_shapes=[pltpu.VMEM((tokens, wide), jnp.bfloat16)],
        ),
        out_shape=[jax.ShapeDtypeStruct((units, width), jnp.bfloat16) for width in cuts],
        compiler_params=params,
        cost_estimate=estimate(2 * units * tokens * wide, units * (columns + wide) * 2),
    )(at, *parts, hidden, weight)


def terms_kernel(scale, at_ref, hidden_ref, weight_ref, keep_ref, send_ref, total_ref):
    def body(rows):
        total_ref[rows, :] = scale * jnp.dot(
            hidden_ref[rows, :], weight_ref[...], preferred_element_type=jnp.float32
        )

    in_rows(total_ref.shape[0], 256, body)
    size = keep_ref.shape[1]
    for chip in range(2):
        for out_ref, mask in ((keep_ref, 2 * chip), (send_ref, 2 * chip + 1)):
            row = pl.multiple_of((at_ref[0] ^ mask) * size, size)
            out_ref[chip] = total_ref[pl.ds(row, size), :]


def make_terms(at, hidden, weight, scale):
    tokens, units = hidden.shape
    features = weight.shape[1]
    size = tokens // 4
    block = pl.BlockSpec((2, size, 512), lambda i, at: (0, 0, i))
    shape = jax.ShapeDtypeStruct((2, size, features), jnp.float32)
    return pl.pallas_call(
        functools.partial(terms_kernel, scale),
        grid_spec=pltpu.PrefetchScalarGridSpec(
            num_scalar_prefetch=1,
            grid=(features // 512,),
            in_specs=[
                pl.BlockSpec((tokens, units), lambda i, at: (0, 0)),
                pl.BlockSpec((units, 512), lambda i, at: (0, i)),
            ],
            out_specs=[block, block],
            scratch_shapes=[pltpu.VMEM((tokens, 512), jnp.float32)],
        ),
        out_shape=[shape, shape],
        compiler_params=params,
        cost_estimate=estimate(2 * units * tokens * features, units * features * 2 + tokens * features * 4),
    )(at, hidden, weight)


def chip_sum_kernel(keep_ref, sibling_ref, out_ref):
    def body(rows):
        out_ref[rows, :] = (keep_ref[0, rows, :] + sibling_ref[0, rows, :]).astype(out_ref.dtype)

    in_rows(out_ref.shape[0], 16, body)


def chip_sum(keep, sibling, kind):
    _, size, features = keep.shape
    block = pl.BlockSpec((1, size, features), lambda i: (1, 0, 0))
    return pl.pallas_call(
        chip_sum_kernel,
        grid=(1,),
        in_specs=[block, block],
        out_specs=pl.BlockSpec((size, features), lambda i: (0, 0)),
        out_shape=jax.ShapeDtypeStruct((size, features), kind),
        compiler_params=params,
        cost_estimate=estimate(size * features, size * features * 12),
    )(keep, sibling)


def last_sum_kernel(keep_ref, sibling_ref, other_ref, out_ref):
    def body(rows):
        total = keep_ref[0, rows, :] + sibling_ref[0, rows, :]
        out_ref[rows, :] = (total + other_ref[rows, :].astype(jnp.float32)).astype(jnp.bfloat16)

    in_rows(out_ref.shape[0], 16, body)


def last_sum(keep, sibling, other):
    _, size, features = keep.shape
    block = pl.BlockSpec((1, size, features), lambda i: (0, 0, 0))
    flat = pl.BlockSpec((size, features), lambda i: (0, 0))
    return pl.pallas_call(
        last_sum_kernel,
        grid=(1,),
        in_specs=[block, block, flat],
        out_specs=flat,
        out_shape=jax.ShapeDtypeStruct((size, features), jnp.bfloat16),
        compiler_params=params,
        cost_estimate=estimate(2 * size * features, size * features * 14),
    )(keep, sibling, other)


def grads_kernel(scale, at_ref, *refs):
    head_refs, rest_refs = refs[:4], refs[4:8]
    weight_ref, gate_ref, up_ref, gate_out, up_out, cot_ref, total_ref = refs[8:]

    @pl.when(pl.program_id(0) == 0)
    def _():
        put_tokens(at_ref, head_refs, cot_ref, 0)
        put_tokens(at_ref, rest_refs, cot_ref, head)

    def product(rows):
        total_ref[rows, :] = scale * lax.dot_general(
            cot_ref[rows, :], weight_ref[...], (((1,), (1,)), ((), ())), preferred_element_type=jnp.float32
        )

    in_rows(total_ref.shape[0], 256, product)

    def body(rows):
        total = total_ref[rows, :]
        gate = gate_ref[rows, :].astype(jnp.float32)
        up = up_ref[rows, :].astype(jnp.float32)
        sig = jax.nn.sigmoid(gate)
        gate_out[rows, :] = (total * up * sig * (1.0 + gate * (1.0 - sig))).astype(jnp.bfloat16)
        up_out[rows, :] = (total * (gate * sig)).astype(jnp.bfloat16)

    in_rows(gate_ref.shape[0], 64, body)


def make_grads(at, head_parts, rest_parts, weight, gate, up, scale):
    tokens, units = gate.shape
    features = weight.shape[1]
    wide = grads_wide
    block = pl.BlockSpec((tokens, wide), lambda i, at: (0, i))
    shape = jax.ShapeDtypeStruct((tokens, units), jnp.bfloat16)
    parts = list(head_parts) + list(rest_parts)
    return pl.pallas_call(
        functools.partial(grads_kernel, scale),
        grid_spec=pltpu.PrefetchScalarGridSpec(
            num_scalar_prefetch=1,
            grid=(units // wide,),
            in_specs=[pl.BlockSpec(part.shape, lambda i, at: (0, 0)) for part in parts]
            + [pl.BlockSpec((wide, features), lambda i, at: (i, 0)), block, block],
            out_specs=[block, block],
            scratch_shapes=[
                pltpu.VMEM((tokens, features), jnp.bfloat16),
                pltpu.VMEM((tokens, wide), jnp.float32),
            ],
        ),
        out_shape=[shape, shape],
        compiler_params=params,
        cost_estimate=estimate(2 * units * tokens * features, units * features * 2 + tokens * units * 8),
    )(at, *parts, weight, gate, up)


def averaged_kernel(own_ref, peer_ref, *refs):
    out_ref = refs[-1]

    def body(rows):
        own = own_ref[rows, :].astype(jnp.float32)
        out_ref[rows, :] = ((own + peer_ref[rows, :].astype(jnp.float32)) * 0.5).astype(jnp.bfloat16)

    in_rows(out_ref.shape[0], 64, body)


def averaged(mixed, own, peer, at, features):
    units, width = own.shape
    run = math.gcd(width, at)
    first = at // run
    block = pl.BlockSpec((units // 2, run), lambda i, j: (i, j))
    before = [] if mixed is None else [mixed]
    return pl.pallas_call(
        averaged_kernel,
        grid=(2, width // run),
        in_specs=[block, block] + [pl.BlockSpec(memory_space=pl.ANY)] * len(before),
        out_specs=pl.BlockSpec((units // 2, run), lambda i, j: (i, first + j)),
        out_shape=jax.ShapeDtypeStruct((units, features), jnp.bfloat16),
        input_output_aliases={2: 0} if before else {},
        compiler_params=params,
        cost_estimate=estimate(units * width * 2, units * width * 6),
    )(own, peer, *before)


def step_with(power, scale, at, gate, up, weight, head_parts, rest_rows, rest_core, hidden, new_head):
    features = weight.shape[1]
    factor = learning_rate * scale
    odd = power in (1, 3)
    if odd:
        head_at, rest_cuts = ((0, 256), (256, 256), (512, 256)), odd_cuts
        mine = [new_head[2], new_head[3], new_head[1]]
        around, order = (2, 3), (0, 1, 2, 5, 4, 3)
    else:
        head_at, rest_cuts = ((0, 512), (512, 256)), even_cuts
        mine = [new_head[0], new_head[1]]
        around, order = (), (0, 2, 3, 4, 1)
    rest_at, column = [], 0
    for width in rest_cuts:
        rest_at.append((column, width))
        column += width
    starts = [lo for lo, _ in head_at] + [head + lo for lo, _ in rest_at]

    def hop(value, piece, count):
        if piece in around:
            return lax.ppermute(value, both, backward_hops(power)[count])
        return lax.ppermute(value, both, direct_pairs(power))

    chip = swapped(rest_rows, 2)
    keep, send = make_terms(at, hidden, weight, scale)
    if power == 0:
        mine[0], chip = lax.optimization_barrier((mine[0], chip))

    hops = {0: hop(mine[0], 0, 0)}
    chip, keep, send = lax.optimization_barrier((chip, keep, send))
    if odd:
        hops[1] = hop(mine[1], 1, 0)
        hops[2] = hop(mine[2], 2, 0)
        hops[0], hops[2], chip = lax.optimization_barrier((hops[0], hops[2], chip))
        hops[2] = hop(hops[2], 2, 1)
    rest_parts = (rest_rows, rest_core, chip, swapped(chip, 1))

    rest = list(make_updated(at, rest_parts, hidden, weight, factor, head, rest_at))
    pieces = mine + rest
    mixed = None
    if odd:
        hops[3] = hop(rest[0], 3, 0)
        hops[5] = hop(rest[2], 5, 0)
        rest[1], gate = lax.optimization_barrier((rest[1], gate))
        grad_gate, grad_up = make_grads(at, head_parts, rest_parts, weight, gate, up, scale)
        hops[1], hops[2], rest[1], send = lax.optimization_barrier((hops[1], hops[2], rest[1], send))
        hops[2] = hop(hops[2], 2, 2)
        hops[4] = hop(rest[1], 4, 0)
        sibling = swapped(send, 1)
        summed = chip_sum(keep, sibling, jnp.float32)
        hops[3], grad_gate = lax.optimization_barrier((hops[3], grad_gate))
        hops[3] = hop(hops[3], 3, 1)
        other = swapped(summed, 2)
        for piece in order[:2]:
            mixed = averaged(mixed, pieces[piece], hops[piece], starts[piece], features)
        hops[2], hops[3], mixed, other = lax.optimization_barrier((hops[2], hops[3], mixed, other))
        hops[3] = hop(hops[3], 3, 2)
        layer_out = last_sum(keep, sibling, other)
        hops[5], layer_out = lax.optimization_barrier((hops[5], layer_out))
        left = order[2:]
    else:
        hops[2] = hop(rest[0], 2, 0)
        hops[0], rest[1], send = lax.optimization_barrier((hops[0], rest[1], send))
        hops[3] = hop(rest[1], 3, 0)
        hops[2], rest[2], gate = lax.optimization_barrier((hops[2], rest[2], gate))
        hops[4] = hop(rest[2], 4, 0)
        hops[1] = hop(mine[1], 1, 0)
        sibling = swapped(send, 1)
        grad_gate, grad_up = make_grads(at, head_parts, rest_parts, weight, gate, up, scale)
        kind = jnp.bfloat16 if power == 0 else jnp.float32
        layer_out = last_sum(keep, sibling, swapped(chip_sum(keep, sibling, kind), 2))
        hops[4], layer_out = lax.optimization_barrier((hops[4], layer_out))
        left = order
    for piece in left:
        mixed = averaged(mixed, pieces[piece], hops[piece], starts[piece], features)
    return layer_out, grad_gate, grad_up, mixed


def per_device(gate_pre, up_pre, down_weight, cotangent, peer_exp):
    gate, up, weight, cot_rows = gate_pre[0], up_pre[0], down_weight[0], cotangent[0]
    width_all = weight.shape[0] * lax.axis_size("tensor")
    scale = float(np.float32(1.0) / np.sqrt(np.float32(width_all)))
    at = lax.axis_index("tensor").astype(jnp.int32).reshape(1)

    rows = cot_rows[:, :head]
    rest_rows = cot_rows[:, head:]
    core = swapped(rows, 1)
    chip = swapped(rows, 2)
    hidden = make_hidden(gate, up)
    chip, hidden, rest_rows = lax.optimization_barrier((chip, hidden, rest_rows))
    head_parts = (rows, core, chip, swapped(chip, 1))
    rest_core = swapped(rest_rows, 1)
    new_head = make_updated(at, head_parts, hidden, weight, learning_rate * scale, 0, head_runs)

    outs = lax.switch(
        jnp.clip(peer_exp[0], 0, 4),
        [functools.partial(step_with, power, scale) for power in range(5)],
        at,
        gate,
        up,
        weight,
        head_parts,
        rest_rows,
        rest_core,
        hidden,
        tuple(new_head),
    )
    return tuple(out[None] for out in outs)


def solution(mesh):
    return jax.shard_map(
        per_device,
        mesh=mesh,
        in_specs=(
            P("replica", None, "tensor"),
            P("replica", None, "tensor"),
            P("replica", "tensor", None),
            P("replica", "tensor", None),
            P(),
        ),
        out_specs=(
            P("replica", "tensor", None),
            P("replica", None, "tensor"),
            P("replica", None, "tensor"),
            P("replica", "tensor", None),
        ),
        check_vma=False,
    )
```
